256 devices in a mesh: replica: 4 (over z_hi), fsdp: 16 (over y, z_lo, core), tensor: 4 (over x).
Axes of the slice: x: 4, y: 4, z: 8 (z_hi: 4, z_lo: 2; z = z_hi * 2 + z_lo), core: 2. Of those that a mesh axis runs over, the one named last changes fastest.
Arguments:
- inputs: bfloat16 [4, 8192, 8192], P('replica', 'fsdp'), may hold values from -6 to 6
- key_grad: bfloat16 [4, 8192, 1024], P('replica', 'fsdp', 'tensor'), may hold values from -0.75 to 0.75
- value_grad: bfloat16 [4, 8192, 1024], P('replica', 'fsdp', 'tensor'), may hold values from -0.75 to 0.75
- key_weight: bfloat16 [4, 8192, 1024], P('replica', 'fsdp', 'tensor'), may hold values from -0.0625 to 0.0625
- value_weight: bfloat16 [4, 8192, 1024], P('replica', 'fsdp', 'tensor'), may hold values from -0.0625 to 0.0625
- global_params: float32 [1024, 8192], P('fsdp', 'tensor'), may hold values from -6 to 6
- momentum: float32 [1024, 8192], P('fsdp', 'tensor'), may hold values from -6 to 6
- local_params: float32 [4, 1024, 8192], P('replica', 'fsdp', 'tensor'), may hold values from -6 to 6
- fragment: int32 [1], replicated, may hold values from 0 to 7
- step: int32 [1], replicated, may hold values from 0 to 127
- outer_rates: float32 [8], replicated, may hold values from 0.3 to 1
Outputs:
- input_grad: bfloat16 [4, 8192, 8192], P('replica', 'fsdp', 'tensor')
- key_wgrad: float32 [4, 8192, 1024], P('replica', 'fsdp', 'tensor')
- value_wgrad: float32 [4, 8192, 1024], P('replica', 'fsdp', 'tensor')
- new_global: float32 [1024, 8192], P('fsdp', 'tensor')
- new_momentum: float32 [1024, 8192], P('fsdp', 'tensor')
- new_local: float32 [4, 1024, 8192], P('replica', 'fsdp', 'tensor')
The draws below stay inside these ranges and needn't reach their ends.
All inputs are finite; a program needn't handle non-finite values.
Results may differ from the reference program's by a relative error of at most 0.0095.
Values may be sent and summed in bfloat16 or wider, within the bound.
No kernel may reach another device: no remote copies, remote signals or barrier semaphores. Data moves between devices by JAX's collectives and lax.ppermute only.
A program may use at most 128 MiB of HBM per device.

```python
import math
import jax
import jax.numpy as jnp
from jax import lax

D = 8192
FRAG_ROWS = 1024
FRAGMENTS = 8
WARMUP = 64
KV = 1024
TOKENS = 8192
REPLICAS = 4


def strengthened(drawn, own_key, source, target, parts, factor):
    def block_of(axis_at):
        return (jnp.arange(drawn.shape[axis_at]) // (drawn.shape[axis_at] // parts)).reshape((-1,) + (1,) * (drawn.ndim - 1 - axis_at))

    near = jax.random.permutation(own_key, parts)[block_of(target)]
    other_side = (block_of(target) + parts // 2) % parts
    return jnp.where((block_of(source) == near) | (block_of(source) == other_side), factor * drawn, drawn)


def block_levels(key, dims, shards, least, high):
    gain = 1.0
    for axis_at, shards_of in shards:
        steps = jax.random.uniform(jax.random.fold_in(jax.random.fold_in(key, 6), axis_at), (shards_of,), jnp.float32, least / len(shards), high / len(shards))
        gain = gain * jnp.repeat(jnp.exp(steps), dims[axis_at] // shards_of).reshape((-1,) + (1,) * (len(dims) - 1 - axis_at))
    return gain


def noise(own_key, dims, scale, limit, pieces=(), kind=jnp.bfloat16):
    level = block_levels(own_key, dims, pieces, -0.22, 0.18) if pieces else 1.0
    array = jax.random.normal(own_key, dims, jnp.float32) * scale * level
    return jnp.minimum(jnp.maximum(array, -limit), limit).astype(kind)


def gaussian_with(rng, extent, spread, bound, pieces, heavy, kind=jnp.bfloat16):
    array = spread * jax.random.normal(rng, extent, jnp.float32)
    if pieces:
        array = array * block_levels(rng, extent, pieces, -0.22, 0.18)
    return jnp.clip(strengthened(array, jax.random.fold_in(rng, 3), *heavy), -bound, bound).astype(kind)


def setup_inputs(seed: int = 0) -> dict:
    key_of = jax.random.split(jax.random.key(seed), 12)
    return {
        "inputs": gaussian_with(key_of[0], (REPLICAS, TOKENS, D), 1.0, 6.0, ((0, 4), (1, 16)), (1, 2, 16, 2.0)),
        "key_grad": noise(key_of[1], (REPLICAS, TOKENS, KV), 0.125, 0.75, ((0, 4), (1, 16), (2, 4))),
        "value_grad": noise(key_of[2], (REPLICAS, TOKENS, KV), 0.125, 0.75, ((0, 4), (1, 16), (2, 4))),
        "key_weight": noise(key_of[3], (REPLICAS, D, KV), D ** -0.5, 0.0625, ((0, 4), (1, 16), (2, 4))),
        "value_weight": noise(key_of[4], (REPLICAS, D, KV), D ** -0.5, 0.0625, ((0, 4), (1, 16), (2, 4))),
        "global_params": noise(key_of[5], (FRAG_ROWS, D), 1.0, 6.0, ((0, 16), (1, 4)), jnp.float32),
        "momentum": noise(key_of[6], (FRAG_ROWS, D), 1.0, 6.0, ((0, 16), (1, 4)), jnp.float32),
        "local_params": noise(key_of[7], (REPLICAS, FRAG_ROWS, D), 1.0, 6.0, ((0, 4), (1, 16), (2, 4)), jnp.float32),
        "fragment": jax.random.randint(key_of[8], (1,), 0, FRAGMENTS).astype(jnp.int32),
        "step": jax.random.randint(key_of[9], (1,), 0, 2 * WARMUP).astype(jnp.int32),
        "outer_rates": jnp.clip(jnp.exp(jax.random.uniform(key_of[10], (FRAGMENTS,), jnp.float32, math.log(0.3), math.log(1.0))), 0.3, 1.0),
    }


momentum_decay = 0.9
mixing = 0.5


def reference(inputs, key_grad, value_grad, key_weight, value_weight, global_params, momentum, local_params, fragment, step, outer_rates):
    def one_replica(items):
        tokens_in, grad_k, grad_v, weight_k, weight_v = items
        back_k = lax.dot_general(grad_k, weight_k, (((1,), (1,)), ((), ())), preferred_element_type=jnp.float32)
        back_v = lax.dot_general(grad_v, weight_v, (((1,), (1,)), ((), ())), preferred_element_type=jnp.float32)
        back = (back_k + back_v).astype(jnp.bfloat16)
        wgrad_k = lax.dot_general(tokens_in, grad_k, (((0,), (0,)), ((), ())), preferred_element_type=jnp.float32)
        wgrad_v = lax.dot_general(tokens_in, grad_v, (((0,), (0,)), ((), ())), preferred_element_type=jnp.float32)
        return back, wgrad_k, wgrad_v

    input_grad, key_wgrad, value_wgrad = lax.map(one_replica, (inputs, key_grad, value_grad, key_weight, value_weight))
    chosen = (jnp.arange(FRAGMENTS, dtype=jnp.int32) == fragment[0]).astype(jnp.float32)
    warm = jnp.minimum(1.0, (step[0].astype(jnp.float32) + 1.0) / WARMUP)
    rate = jnp.sum(chosen * outer_rates) * warm
    average = jnp.sum(local_params, axis=0) / REPLICAS
    delta = global_params - average
    new_momentum = momentum_decay * momentum + delta
    new_global = global_params - rate * (delta + momentum_decay * new_momentum)
    new_local = mixing * local_params + (1.0 - mixing) * new_global[None]
    return input_grad, key_wgrad, value_wgrad, new_global, new_momentum, new_local
```

```python
import jax
import jax.numpy as jnp
from jax import lax
from jax.experimental import pallas as pl
from jax.experimental.pallas import tpu as pltpu
from jax.sharding import Mesh, PartitionSpec as P

WARMUP = 64


momentum_decay = 0.9
mixing = 0.5
bf16 = jnp.bfloat16
f32 = jnp.float32
VMEM_LIMIT = 16 * 1024 * 1024


def shift(a, axis, by):
    n = lax.axis_size(axis)
    return lax.ppermute(a, axis, [(i, (i + by) % n) for i in range(n)])


def outer_step(global_part, momentum_part, average, rate):
    delta = global_part - average
    fresh_momentum = momentum_decay * momentum_part + delta
    fresh_global = global_part - rate * (delta + momentum_decay * fresh_momentum)
    return (fresh_global, fresh_momentum)


fence = lax.optimization_barrier
VMEM_SPEC = pl.BlockSpec(memory_space=pltpu.VMEM)
HBM_SPEC = pl.BlockSpec(memory_space=pltpu.HBM)
SMEM_SPEC = pl.BlockSpec(memory_space=pltpu.SMEM)


def call(kernel, where, ins, outs, scratch=(), far=(), aliases=None, flops=0):
    moved = sum(a.size * a.dtype.itemsize for a in list(ins) + list(outs))
    n_in = len(ins)
    spaces = [pltpu.HBM if k in far else pltpu.VMEM for k in range(n_in + len(outs))]
    specs = [HBM_SPEC if space is pltpu.HBM else VMEM_SPEC for space in spaces]
    placed = [pltpu.with_memory_space_constraint(a, space) for a, space in zip(ins, spaces)]
    return pl.pallas_call(
        kernel,
        out_shape=[space(a.shape, a.dtype) for a, space in zip(outs, spaces[n_in:])],
        in_specs=[SMEM_SPEC] + specs[:n_in],
        out_specs=specs[n_in:],
        scratch_shapes=list(scratch),
        input_output_aliases=aliases or {},
        compiler_params=pltpu.CompilerParams(vmem_limit_bytes=VMEM_LIMIT),
        cost_estimate=pl.CostEstimate(flops=flops, bytes_accessed=moved, transcendentals=0),
    )(where, *placed)


def like(*shape, dtype=bf16):
    return jax.ShapeDtypeStruct(shape, dtype)


def started(src, dst, sem):
    copy = pltpu.make_async_copy(src, dst, sem)
    copy.start()
    return copy


def column(ref, index, width):
    return ref.at[:, pl.ds(pl.multiple_of(index * width, width), width)]


def join_kernel(_, a, b, out, sems):
    width = a.shape[1]
    copies = [started(a, out.at[:, :width], sems.at[0]), started(b, out.at[:, width:], sems.at[1])]
    for copy in copies:
        copy.wait()


def join(none, a, b):
    rows, width = a.shape
    return call(join_kernel, none, [a, b], [like(rows, 2 * width)], [pltpu.SemaphoreType.DMA((2,))], far=(0, 1))[0]


def pack_kernel(where, x, grads, out, sems):
    width = out.shape[2]
    copies = [started(column(x, where[i], width), out.at[i], sems.at[i]) for i in range(8)]
    out[8] = grads[...]
    for copy in copies:
        copy.wait()


def pack_columns(where, tokens_in, grads):
    rows, width = grads.shape
    return call(
        pack_kernel, where, [tokens_in, grads], [like(9, rows, width)], [pltpu.SemaphoreType.DMA((8,))], far=(0,)
    )[0]


def partial_kernel(where, x, grads, pack, up, down, far, own, x_buf, sems):
    width = grads.shape[1]

    def load(i):
        return started(column(x, where[i], width), x_buf.at[i % 3], sems.at[i % 3])

    loads = [load(0), load(1)]
    for i in range(8):
        if i < 6:
            loads.append(load(i + 2))
        loads[i].wait()
        acc = lax.dot_general(grads[...], x_buf[i % 3], (((0,), (0,)), ((), ())), preferred_element_type=f32)
        acc = acc + lax.dot_general(pack[8], pack[i], (((0,), (0,)), ((), ())), preferred_element_type=f32)
        (up, down, far, own)[i // 2][i % 2] = acc.astype(bf16)


def partials(where, tokens_in, grads, pack):
    rows, width = grads.shape
    return call(
        partial_kernel,
        where,
        [tokens_in, grads, pack],
        [like(2, width, width)] * 4,
        [pltpu.VMEM((3, rows, width), bf16), pltpu.SemaphoreType.DMA((3,))],
        far=(0,),
        flops=32 * rows * width * width,
    )


def pick_kernel(where, *refs):
    held, outs = refs[:4], refs[4:]
    for s in range(4):
        for d in range(4):
            @pl.when((where[0] + s) % 4 == d)
            def _(s=s, d=d):
                outs[s][...] = held[d][...]


def pick(turn, held):
    return call(pick_kernel, turn, held, [like(*held[0].shape)] * 4)


def back_kernel(where, *refs):
    heads, heads_sib, weights, (out, sib_out, o_buf, sem) = refs[:4], refs[4:8], refs[8:12], refs[-4:]
    width = o_buf.shape[1]

    def product(lhs):
        acc = None
        for g, w in zip(lhs, weights):
            part = lax.dot_general(g[...], w[...], (((1,), (1,)), ((), ())), preferred_element_type=f32)
            acc = part if acc is None else acc + part
        return acc.astype(bf16)

    o_buf[...] = product(heads)
    kept = started(o_buf, column(out, where[0], width), sem)
    sib_out[...] = product(heads_sib)
    kept.wait()


def back_block(where, heads, heads_sib, weights, so_far):
    tokens, width = heads[0].shape
    ins = [*heads, *heads_sib, *weights] + ([] if so_far is None else [so_far])
    n = len(ins)
    return call(
        back_kernel,
        where,
        ins,
        [like(tokens, 4 * width), like(tokens, width)],
        [pltpu.VMEM((tokens, width), bf16), pltpu.SemaphoreType.DMA],
        far=(12, n),
        aliases={} if so_far is None else {13: 0},
        flops=16 * tokens * width * width,
    )


def place_kernel(where, a, b, _, out, sems):
    width = a.shape[1]
    copies = [started(src, column(out, where[k], width), sems.at[k]) for k, src in enumerate((a, b))]
    for copy in copies:
        copy.wait()


def place(where, a, b, back):
    return call(
        place_kernel, where, [a, b, back], [like(*back.shape)], [pltpu.SemaphoreType.DMA((2,))], far=(2, 3), aliases={3: 0}
    )[0]


def other_kernel(_, a, b, c, d, out):
    out[...] = (a[0].astype(f32) + b[0].astype(f32) + c[0].astype(f32) + d[0].astype(f32)).astype(bf16)


def other_sum(none, parts):
    return call(other_kernel, none, parts, [like(*parts[0].shape[1:])])[0]


def mine_kernel(_, a, b, c, d, e, key_out, value_out, k_buf, v_buf, sems):
    width = k_buf.shape[1]

    def total(rows):
        return sum(ref[1, rows].astype(f32) for ref in (a, b, c, d)) + e[rows].astype(f32)

    k_buf[...] = total(slice(0, width)).T
    first = started(k_buf, key_out, sems.at[0])
    v_buf[...] = total(slice(width, 2 * width)).T
    started(v_buf, value_out, sems.at[1]).wait()
    first.wait()


def mine_sum(none, parts, received):
    _, rows, cols = parts[0].shape
    half = (cols, rows // 2)
    return call(
        mine_kernel,
        none,
        [*parts, received],
        [like(*half, dtype=f32)] * 2,
        [pltpu.VMEM(half, f32), pltpu.VMEM(half, f32), pltpu.SemaphoreType.DMA((2,))],
        far=(5, 6),
    )


def local(
    inputs,
    key_grad,
    value_grad,
    key_weight,
    value_weight,
    global_params,
    momentum,
    local_params,
    fragment,
    step,
    outer_rates,
):
    iy, iz, ic, ix = (lax.axis_index(a).astype(jnp.int32) for a in ("y", "z", "c", "x"))
    none = jnp.zeros((1,), jnp.int32)
    tokens_in = inputs[0]
    base = jnp.stack([((iy + d) % 4) * 4 + z * 2 for d in (1, 3, 2, 0) for z in (1 - iz, iz)])
    local_now = local_params[0]
    sent = local_now.astype(bf16)

    weight = join(none, key_weight[0], value_weight[0])
    w1, w3 = shift(weight, "y", -1), shift(weight, "y", -3)
    grads = join(none, key_grad[0], value_grad[0])
    pack = shift(pack_columns(base + 1 - ic, tokens_in, grads), "c", 1)
    r1, r3 = shift(sent, "r", 1), shift(sent, "r", 3)

    pack, sent_b, grads_b, w1, w3, weight_b = fence((pack, sent, grads, w1, w3, weight))
    parts = partials(base + ic, tokens_in, grads, pack)
    grads_sib = pack[8]
    w2 = shift(weight_b, "y", 2)
    h1, h3 = shift(grads_b, "x", 1), shift(grads_b, "x", 3)
    r2 = shift(sent_b, "r", 2)

    w2, w1, w3, parts, h1, h3, r1, r2, r3 = fence((w2, w1, w3, parts, h1, h3, r1, r2, r3))
    near0, pick1, pick2, pick3 = pick(((ix - iy) % 4).reshape(1), [weight, w1, w2, w3])
    near1, near3 = shift(pick1, "x", 1), shift(pick3, "x", 3)
    over0 = shift(near0, "z", 1)
    up, down, far, own = parts
    up, down = shift(up, "y", 1), shift(down, "y", 3)

    near1, near3, over0, pick2, h1 = fence((near1, near3, over0, pick2, h1))
    near2 = shift(pick2, "x", 2)
    over1 = shift(near1, "z", 1)
    h1c = shift(h1, "c", 1)

    near2, over1, up, down, h1c, grads_f, h3, near3, far = fence((near2, over1, up, down, h1c, grads, h3, near3, far))
    over3 = shift(near3, "z", 1)
    far = shift(far, "y", 2)
    h2 = shift(grads_f, "x", 2)
    h3c = shift(h3, "c", 1)

    over3, h2, h3c, near2 = fence((over3, h2, h3c, near2))
    over2 = shift(near2, "z", 1)
    h2c = shift(h2, "c", 1)
    heads, heads_sib = [grads, h1, h2, h3], [grads_sib, h1c, h2c, h3c]
    back, near_out = back_block((iz * 2 + ic).reshape(1), heads, heads_sib, [near0, near1, near2, near3], None)

    over2, far, back, near_out = fence((over2, far, back, near_out))
    parts = [up, down, far, own]
    received = shift(other_sum(none, parts), "z", 1)
    near_out = shift(near_out, "c", 1)
    back, over_out = back_block(((1 - iz) * 2 + ic).reshape(1), heads, heads_sib, [over0, over1, over2, over3], back)
    over_out = shift(over_out, "c", 1)
    back = place(jnp.stack([iz * 2 + 1 - ic, (1 - iz) * 2 + 1 - ic]), near_out, over_out, back)
    wgrad_k, wgrad_v = mine_sum(none, parts, received)

    total = sent.astype(f32) + r1.astype(f32) + r2.astype(f32) + r3.astype(f32)
    count_frag = outer_rates.shape[0]
    chosen = (jnp.arange(count_frag, dtype=jnp.int32) == fragment[0]).astype(f32)
    warm = jnp.minimum(1.0, (step[0].astype(f32) + 1.0) / WARMUP)
    rate = jnp.sum(chosen * outer_rates) * warm
    replicas = lax.axis_size("r")
    fresh_global, fresh_momentum = outer_step(global_params, momentum, total / replicas, rate)
    fresh_local = mixing * local_now + (1.0 - mixing) * fresh_global
    return (
        back[None],
        wgrad_k[None],
        wgrad_v[None],
        fresh_global,
        fresh_momentum,
        fresh_local[None],
    )


def solution(mesh):
    fine = Mesh(mesh.devices.reshape(4, 4, 2, 2, 4), ("r", "y", "z", "c", "x"))
    fsdp = ("y", "z", "c")
    split = P("r", fsdp, "x")
    in_specs = (
        P("r", fsdp, None),
        split,
        split,
        split,
        split,
        P(fsdp, "x"),
        P(fsdp, "x"),
        split,
        P(),
        P(),
        P(),
    )
    out_specs = (split, split, split, P(fsdp, "x"), P(fsdp, "x"), split)
    return jax.shard_map(local, mesh=fine, in_specs=in_specs, out_specs=out_specs, check_vma=False)
```

```python
import jax
import jax.numpy as jnp
from jax import lax
from jax.experimental import pallas as pl
from jax.experimental.pallas import tpu as pltpu
from jax.sharding import Mesh, PartitionSpec as P

WARMUP = 64


momentum_decay = 0.9
mixing = 0.5
bf16 = jnp.bfloat16
f32 = jnp.float32
VMEM_LIMIT = 16 * 1024 * 1024


def shift(a, axis, by):
    n = lax.axis_size(axis)
    return lax.ppermute(a, axis, [(i, (i + by) % n) for i in range(n)])


def outer_step(global_part, momentum_part, average, rate):
    delta = global_part - average
    fresh_momentum = momentum_decay * momentum_part + delta
    fresh_global = global_part - rate * (delta + momentum_decay * fresh_momentum)
    return (fresh_global, fresh_momentum)


fence = lax.optimization_barrier
VMEM_SPEC = pl.BlockSpec(memory_space=pltpu.VMEM)
HBM_SPEC = pl.BlockSpec(memory_space=pltpu.HBM)
SMEM_SPEC = pl.BlockSpec(memory_space=pltpu.SMEM)


def call(kernel, where, ins, outs, scratch=(), far=(), aliases=None, flops=0):
    n_in = len(ins)
    spaces = [pltpu.HBM if k in far else pltpu.VMEM for k in range(n_in + len(outs))]
    specs = [HBM_SPEC if space is pltpu.HBM else VMEM_SPEC for space in spaces]
    placed = [pltpu.with_memory_space_constraint(a, space) for a, space in zip(ins, spaces)]
    return pl.pallas_call(
        kernel,
        out_shape=[space(a.shape, a.dtype) for a, space in zip(outs, spaces[n_in:])],
        in_specs=[SMEM_SPEC] + specs[:n_in],
        out_specs=specs[n_in:],
        scratch_shapes=list(scratch),
        input_output_aliases=aliases or {},
        compiler_params=pltpu.CompilerParams(vmem_limit_bytes=VMEM_LIMIT),
        cost_estimate=pl.CostEstimate(flops=flops, bytes_accessed=0, transcendentals=0),
    )(where, *placed)


def like(*shape, dtype=bf16):
    return jax.ShapeDtypeStruct(shape, dtype)


def started(src, dst, sem):
    copy = pltpu.make_async_copy(src, dst, sem)
    copy.start()
    return copy


def column(ref, index, width):
    return ref.at[:, pl.ds(pl.multiple_of(index * width, width), width)]


def join_kernel(_, a, b, out, sems):
    width = a.shape[1]
    copies = [started(a, out.at[:, :width], sems.at[0]), started(b, out.at[:, width:], sems.at[1])]
    for copy in copies:
        copy.wait()


def join(none, a, b):
    rows, width = a.shape
    return call(join_kernel, none, [a, b], [like(rows, 2 * width)], [pltpu.SemaphoreType.DMA((2,))], far=(0, 1))[0]


def prepare_kernel(where, x, gk, gv, grads, pack, sems):
    width = gk.shape[1]
    block = pack.shape[2]
    count = pack.shape[0] - 1
    joined = [started(gk, grads.at[:, :width], sems.at[0]), started(gv, grads.at[:, width:], sems.at[1])]
    copies = [started(column(x, where[i], block), pack.at[i], sems.at[2 + i]) for i in range(count)]
    for copy in joined:
        copy.wait()
    pack[count] = grads[...]
    for copy in copies:
        copy.wait()


def prepare(where, tokens_in, gk, gv):
    rows, width = gk.shape
    count = where.shape[0]
    outs = [like(rows, 2 * width), like(count + 1, rows, 2 * width)]
    return call(prepare_kernel, where, [tokens_in, gk, gv], outs, [pltpu.SemaphoreType.DMA((2 + count,))], far=(0, 1, 2))


def partial_kernel(where, x, grads, pack, *refs):
    pairs, sib_out, (x_buf, sems) = refs[:-3], refs[-3], refs[-2:]
    width = grads.shape[1]
    outs = [ref.at[k] for ref in pairs for k in range(2)]
    sib = pack.at[len(outs)]

    def load(i):
        return started(column(x, where[i], width), x_buf.at[i % 3], sems.at[i % 3])

    loads = [load(i) for i in range(2)]
    for i, out in enumerate(outs):
        if i + 2 < len(outs):
            loads.append(load(i + 2))
        loads[i].wait()
        acc = lax.dot_general(grads[...], x_buf[i % 3], (((0,), (0,)), ((), ())), preferred_element_type=f32)
        acc = acc + lax.dot_general(sib[...], pack[i], (((0,), (0,)), ((), ())), preferred_element_type=f32)
        out[...] = acc.astype(bf16)
    sib_out[...] = sib[...]


def partials(where, tokens_in, grads, pack):
    rows, width = grads.shape
    return call(
        partial_kernel,
        where,
        [tokens_in, grads, pack],
        [like(2, width, width)] * 4 + [like(rows, width)],
        [pltpu.VMEM((3, rows, width), bf16), pltpu.SemaphoreType.DMA((3,))],
        far=(0,),
        flops=32 * rows * width * width,
    )


def pick_kernel(where, *refs):
    held, outs = refs[:4], refs[4:]
    for s in range(4):
        for d in range(4):
            @pl.when((where[0] + s) % 4 == d)
            def _(s=s, d=d):
                outs[s][...] = held[d][...]


def pick(turn, held):
    return call(pick_kernel, turn, held, [like(*held[0].shape)] * 4)


def product(lhs, rhs):
    return lax.dot_general(lhs[...], rhs[...], (((1,), (1,)), ((), ())), preferred_element_type=f32)


def early_kernel(_, *refs):
    own, sib, weights = refs[0:2], refs[2:4], refs[4:6]
    own_acc, sib_acc, buf, sems = refs[6:]
    order = [group[k] for k in range(2) for group in (weights, own, sib)]
    copies = [started(src, buf.at[i], sems.at[i]) for i, src in enumerate(order)]
    for k in range(2):
        for j, acc in enumerate((None, own_acc, sib_acc)):
            copies[3 * k + j].wait()
            if acc is not None:
                part = product(buf.at[3 * k + j], buf.at[3 * k])
                acc[...] = part if k == 0 else acc[...] + part


def early_slots(none, own, sib, weights):
    tokens, width = own[0].shape
    return call(
        early_kernel,
        none,
        [*own, *sib, *weights],
        [like(tokens, width, dtype=f32)] * 2,
        [pltpu.VMEM((6, tokens, width), bf16), pltpu.SemaphoreType.DMA((6,))],
        far=(0, 1, 2, 4, 5),
        flops=8 * tokens * width * width,
    )


def late_slots(refs, accs, w_buf, a_buf, sems, emit):
    heads, blocks = refs[0:2], (refs[2:4], refs[4:6])
    copies = [
        (started(block[0], w_buf.at[k], sems.at[0, k]), started(acc, a_buf.at[k], sems.at[1, k]))
        for k, (block, acc) in enumerate(zip(blocks, accs))
    ]
    for k, block in enumerate(blocks):
        part = product(heads[1], block[1])
        for copy in copies[k]:
            copy.wait()
        emit(k, (a_buf[k] + product(heads[0], w_buf.at[k]) + part).astype(bf16))


def late_scratch(acc):
    return [pltpu.VMEM((2, *acc.shape), bf16), pltpu.VMEM((2, *acc.shape), f32), pltpu.SemaphoreType.DMA((2, 2))]


def loose_kernel(_, *refs):
    out = refs[8]

    def emit(k, block):
        out[k] = block

    late_slots(refs[:6], refs[6:8], *refs[9:], emit)


def loose_blocks(none, heads, near, over, accs):
    ins = [*heads, *near, *over, *accs]
    return call(loose_kernel, none, ins, [like(2, *accs[0].shape)], late_scratch(accs[0]), far=(2, 4, 6, 7))[0]


def back_kernel(where, *refs):
    out, buf, out_sems = refs[8], refs[9], refs[10]
    copies = []

    def emit(k, block):
        buf[k] = block
        copies.append(started(buf.at[k], column(out, where[k], buf.shape[2]), out_sems.at[k]))

    late_slots(refs[:6], refs[6:8], *refs[11:], emit)
    for copy in copies:
        copy.wait()


def back_blocks(where, heads, near, over, accs):
    tokens, width = accs[0].shape
    ins = [*heads, *near, *over, *accs]
    scratch = [pltpu.VMEM((2, tokens, width), bf16), pltpu.SemaphoreType.DMA((2,))] + late_scratch(accs[0])
    return call(back_kernel, where, ins, [like(tokens, 4 * width)], scratch, far=(2, 4, 6, 7, 8))[0]


def place_kernel(where, blocks, _, out, sems):
    width = blocks.shape[2]
    copies = [started(blocks.at[k], column(out, where[k], width), sems.at[k]) for k in range(2)]
    for copy in copies:
        copy.wait()


def place(where, blocks, back):
    return call(
        place_kernel, where, [blocks, back], [like(*back.shape)], [pltpu.SemaphoreType.DMA((2,))], far=(1, 2), aliases={2: 0}
    )[0]


def relay_kernel(_, rest, up, down, first, second):
    first[...] = (rest[0].astype(f32) + up[0].astype(f32)).astype(bf16)
    second[...] = (rest[1].astype(f32) + down[0].astype(f32)).astype(bf16)


def other_kernel(_, own, up, down, out):
    out[...] = (own[0].astype(f32) + up[...].astype(f32) + down[1].astype(f32)).astype(bf16)


def mine_kernel(_, own, up, down, out):
    out[...] = (own[1].astype(f32) + up[1].astype(f32) + down[...].astype(f32)).T


def final_kernel(_, part, received, key_out, value_out, k_buf, v_buf, sems):
    width = k_buf.shape[1]
    k_buf[...] = part[:, :width] + received[:width].astype(f32).T
    first = started(k_buf, key_out, sems.at[0])
    v_buf[...] = part[:, width:] + received[width:].astype(f32).T
    started(v_buf, value_out, sems.at[1]).wait()
    first.wait()


def final_sum(none, part, received):
    rows, cols = received.shape
    half = (cols, rows // 2)
    return call(
        final_kernel,
        none,
        [part, received],
        [like(*half, dtype=f32)] * 2,
        [pltpu.VMEM(half, f32), pltpu.VMEM(half, f32), pltpu.SemaphoreType.DMA((2,))],
        far=(2, 3),
    )


def local(
    inputs,
    key_grad,
    value_grad,
    key_weight,
    value_weight,
    global_params,
    momentum,
    local_params,
    fragment,
    step,
    outer_rates,
):
    iy, iz, ic, ix = (lax.axis_index(a).astype(jnp.int32) for a in ("y", "z", "c", "x"))
    none = jnp.zeros((1,), jnp.int32)
    tokens_in = inputs[0]
    local_now = local_params[0]
    base = jnp.stack([
        ((iy + d) % 4) * 4 + z * 2
        for d, z in ((2, 1 - iz), (1, iz), (2, iz), (3, 1 - iz), (1, 1 - iz), (3, iz), (0, 1 - iz), (0, iz))
    ])

    weight = join(none, key_weight[0], value_weight[0])
    weight, key_part, value_part = fence((weight, key_grad[0], value_grad[0]))
    w1, w3, w2 = shift(weight, "y", -1), shift(weight, "y", -3), shift(weight, "y", 2)
    grads, pack = prepare(base + 1 - ic, tokens_in, key_part, value_part)
    pack = shift(pack, "c", 1)
    sent = local_now.astype(bf16)
    pair_sib = lax.ppermute(sent, "r", [(k, k ^ 1) for k in range(4)])

    pack, grads_b = fence((pack, grads))
    going_up, going_down, relayed, own, sib = partials(base + ic, tokens_in, grads, pack)
    h1 = shift(grads_b, "x", 1)
    pair = (sent.astype(f32) + pair_sib.astype(f32)).astype(bf16)
    pair_sib = lax.ppermute(pair, "r", [(k, k ^ 3) for k in range(4)])

    w1, w2, w3, h1, going_up, going_down = fence((w1, w2, w3, h1, going_up, going_down))
    near0, pick1, pick2, pick3 = pick(((ix - iy) % 4).reshape(1), [weight, w1, w2, w3])
    near1, near3 = shift(pick1, "x", 1), shift(pick3, "x", 3)
    over0 = shift(near0, "z", 1)
    up, down = shift(going_up, "y", 1), shift(going_down, "y", 3)

    near1, near3, over0, pick2, pair_sib = fence((near1, near3, over0, pick2, pair_sib))
    near2 = shift(pick2, "x", 2)
    over1, over3 = shift(near1, "z", 1), shift(near3, "z", 1)

    near2, up, down, over1, grads_f = fence((near2, up, down, over1, grads))
    up_o, down_m = call(relay_kernel, none, [relayed, up, down], [like(*up.shape[1:])] * 2)
    up_o, down_m = shift(up_o, "y", 1), shift(down_m, "y", 3)
    over2 = shift(near2, "z", 1)
    h3, h2 = shift(grads_f, "x", 3), shift(grads_f, "x", 2)
    own_heads, sib_heads = [grads, h1], [sib, shift(h1, "c", 1)]
    near_own, near_sib = early_slots(none, own_heads, sib_heads, [near0, near1])
    over_own, over_sib = early_slots(none, own_heads, sib_heads, [over0, over1])
    up_o, down_m, near_own, near_sib, over_own, over_sib = fence((up_o, down_m, near_own, near_sib, over_own, over_sib))
    other = call(other_kernel, none, [own, up_o, down], [like(*own.shape[1:])])[0]
    received = shift(other, "z", 1)

    h3, h2, over3, over2, other = fence((h3, h2, over3, over2, other))
    heads, near, over = [h3, h2], [near3, near2], [over3, over2]
    loose = loose_blocks(none, [shift(h, "c", 1) for h in heads], near, over, [near_sib, over_sib])
    loose = shift(loose, "c", 1)
    back = back_blocks(jnp.stack([iz * 2 + ic, (1 - iz) * 2 + ic]), heads, near, over, [near_own, over_own])
    mine = call(mine_kernel, none, [own, up, down_m], [like(own.shape[2], own.shape[1], dtype=f32)])[0]
    back = place(jnp.stack([iz * 2 + 1 - ic, (1 - iz) * 2 + 1 - ic]), loose, back)
    back, mine, received = fence((back, mine, received))
    wgrad_k, wgrad_v = final_sum(none, mine, received)

    total = pair.astype(f32) + pair_sib.astype(f32)
    count_frag = outer_rates.shape[0]
    chosen = (jnp.arange(count_frag, dtype=jnp.int32) == fragment[0]).astype(f32)
    warm = jnp.minimum(1.0, (step[0].astype(f32) + 1.0) / WARMUP)
    rate = jnp.sum(chosen * outer_rates) * warm
    replicas = lax.axis_size("r")
    fresh_global, fresh_momentum = outer_step(global_params, momentum, total / replicas, rate)
    fresh_local = mixing * local_now + (1.0 - mixing) * fresh_global
    return (
        back[None],
        wgrad_k[None],
        wgrad_v[None],
        fresh_global,
        fresh_momentum,
        fresh_local[None],
    )


def solution(mesh):
    fine = Mesh(mesh.devices.reshape(4, 4, 2, 2, 4), ("r", "y", "z", "c", "x"))
    fsdp = ("y", "z", "c")
    split = P("r", fsdp, "x")
    in_specs = (
        P("r", fsdp, None),
        split,
        split,
        split,
        split,
        P(fsdp, "x"),
        P(fsdp, "x"),
        split,
        P(),
        P(),
        P(),
    )
    out_specs = (split, split, split, P(fsdp, "x"), P(fsdp, "x"), split)
    return jax.shard_map(local, mesh=fine, in_specs=in_specs, out_specs=out_specs, check_vma=False)
```

```python
import jax
import jax.numpy as jnp
from jax import lax
from jax.experimental import pallas as pl
from jax.experimental.pallas import tpu as pltpu
from jax.sharding import Mesh, PartitionSpec as P

WARMUP = 64


momentum_decay = 0.9
mixing = 0.5
bf16 = jnp.bfloat16
f32 = jnp.float32
VMEM_LIMIT = 16 * 1024 * 1024


def shift(a, axis, by):
    n = lax.axis_size(axis)
    return lax.ppermute(a, axis, [(i, (i + by) % n) for i in range(n)])


def outer_step(global_part, momentum_part, average, rate):
    delta = global_part - average
    fresh_momentum = momentum_decay * momentum_part + delta
    fresh_global = global_part - rate * (delta + momentum_decay * fresh_momentum)
    return (fresh_global, fresh_momentum)


fence = lax.optimization_barrier
VMEM_SPEC = pl.BlockSpec(memory_space=pltpu.VMEM)
HBM_SPEC = pl.BlockSpec(memory_space=pltpu.HBM)
SMEM_SPEC = pl.BlockSpec(memory_space=pltpu.SMEM)


def call(kernel, where, ins, outs, scratch=(), far=(), aliases=None, flops=0):
    n_in = len(ins)
    spaces = [pltpu.HBM if k in far else pltpu.VMEM for k in range(n_in + len(outs))]
    specs = [HBM_SPEC if space is pltpu.HBM else VMEM_SPEC for space in spaces]
    placed = [pltpu.with_memory_space_constraint(a, space) for a, space in zip(ins, spaces)]
    return pl.pallas_call(
        kernel,
        out_shape=[space(a.shape, a.dtype) for a, space in zip(outs, spaces[n_in:])],
        in_specs=[SMEM_SPEC] + specs[:n_in],
        out_specs=specs[n_in:],
        scratch_shapes=list(scratch),
        input_output_aliases=aliases or {},
        compiler_params=pltpu.CompilerParams(vmem_limit_bytes=VMEM_LIMIT),
        cost_estimate=pl.CostEstimate(flops=flops, bytes_accessed=0, transcendentals=0),
    )(where, *placed)


def like(*shape, dtype=bf16):
    return jax.ShapeDtypeStruct(shape, dtype)


def started(src, dst, sem):
    copy = pltpu.make_async_copy(src, dst, sem)
    copy.start()
    return copy


def column(ref, index, width):
    return ref.at[:, pl.ds(pl.multiple_of(index * width, width), width)]


def join_kernel(_, a, b, out, sems):
    width = a.shape[1]
    copies = [started(a, out.at[:, :width], sems.at[0]), started(b, out.at[:, width:], sems.at[1])]
    for copy in copies:
        copy.wait()


def join(none, a, b):
    rows, width = a.shape
    return call(join_kernel, none, [a, b], [like(rows, 2 * width)], [pltpu.SemaphoreType.DMA((2,))], far=(0, 1))[0]


def prepare_kernel(where, x, gk, gv, grads, pack, sems):
    width = gk.shape[1]
    block = pack.shape[2]
    count = pack.shape[0] - 1
    joined = [started(gk, grads.at[:, :width], sems.at[0]), started(gv, grads.at[:, width:], sems.at[1])]
    copies = [started(column(x, where[i], block), pack.at[i], sems.at[2 + i]) for i in range(count)]
    for copy in joined:
        copy.wait()
    pack[count] = grads[...]
    for copy in copies:
        copy.wait()


def prepare(where, tokens_in, gk, gv):
    rows, width = gk.shape
    count = where.shape[0]
    outs = [like(rows, 2 * width), like(count + 1, rows, 2 * width)]
    return call(prepare_kernel, where, [tokens_in, gk, gv], outs, [pltpu.SemaphoreType.DMA((2 + count,))], far=(0, 1, 2))


def partial_kernel(where, x, grads, pack, *refs):
    pairs, sib_out, (x_buf, sems) = refs[:-3], refs[-3], refs[-2:]
    width = grads.shape[1]
    outs = [ref.at[k] for ref in pairs for k in range(2)]
    sib = pack.at[len(outs)]

    def load(i):
        return started(column(x, where[i], width), x_buf.at[i % 3], sems.at[i % 3])

    loads = [load(i) for i in range(2)]
    for i, out in enumerate(outs):
        if i + 2 < len(outs):
            loads.append(load(i + 2))
        loads[i].wait()
        acc = lax.dot_general(grads[...], x_buf[i % 3], (((0,), (0,)), ((), ())), preferred_element_type=f32)
        acc = acc + lax.dot_general(sib[...], pack[i], (((0,), (0,)), ((), ())), preferred_element_type=f32)
        out[...] = acc.astype(bf16)
    sib_out[...] = sib[...]


def partials(where, tokens_in, grads, pack):
    rows, width = grads.shape
    return call(
        partial_kernel,
        where,
        [tokens_in, grads, pack],
        [like(2, width, width)] * 4 + [like(rows, width)],
        [pltpu.VMEM((3, rows, width), bf16), pltpu.SemaphoreType.DMA((3,))],
        far=(0,),
        flops=32 * rows * width * width,
    )


def pick_kernel(where, *refs):
    held, outs = refs[:4], refs[4:]
    for s in range(4):
        for d in range(4):
            @pl.when((where[0] + s) % 4 == d)
            def _(s=s, d=d):
                outs[s][...] = held[d][...]


def pick(turn, held):
    return call(pick_kernel, turn, held, [like(*held[0].shape)] * 4)


def product(lhs, rhs):
    return lax.dot_general(lhs[...], rhs[...], (((1,), (1,)), ((), ())), preferred_element_type=f32)


def early_kernel(_, *refs):
    own, sib, weights = refs[0:2], refs[2:4], refs[4:6]
    own_acc, sib_acc, buf, sems = refs[6:]
    order = [group[k] for k in range(2) for group in (weights, own, sib)]
    copies = [started(src, buf.at[i], sems.at[i]) for i, src in enumerate(order)]
    for k in range(2):
        for j, acc in enumerate((None, own_acc, sib_acc)):
            copies[3 * k + j].wait()
            if acc is not None:
                part = product(buf.at[3 * k + j], buf.at[3 * k])
                acc[...] = part if k == 0 else acc[...] + part


def early_slots(none, own, sib, weights):
    tokens, width = own[0].shape
    return call(
        early_kernel,
        none,
        [*own, *sib, *weights],
        [like(tokens, width, dtype=f32)] * 2,
        [pltpu.VMEM((6, tokens, width), bf16), pltpu.SemaphoreType.DMA((6,))],
        far=(0, 1, 2, 4, 5),
        flops=8 * tokens * width * width,
    )


def late_slots(refs, accs, w_buf, a_buf, sems, emit):
    heads, blocks = refs[0:2], (refs[2:4], refs[4:6])
    copies = [
        (started(block[0], w_buf.at[k], sems.at[0, k]), started(acc, a_buf.at[k], sems.at[1, k]))
        for k, (block, acc) in enumerate(zip(blocks, accs))
    ]
    for k, block in enumerate(blocks):
        part = product(heads[1], block[1])
        for copy in copies[k]:
            copy.wait()
        emit(k, (a_buf[k] + product(heads[0], w_buf.at[k]) + part).astype(bf16))


def late_scratch(acc):
    return [pltpu.VMEM((2, *acc.shape), bf16), pltpu.VMEM((2, *acc.shape), f32), pltpu.SemaphoreType.DMA((2, 2))]


def loose_kernel(_, *refs):
    def emit(k, block):
        refs[8 + k][...] = block

    late_slots(refs[:6], refs[6:8], *refs[10:], emit)


def loose_blocks(none, heads, near, over, accs):
    ins = [*heads, *near, *over, *accs]
    return call(loose_kernel, none, ins, [like(*accs[0].shape)] * 2, late_scratch(accs[0]), far=(2, 4, 6, 7))


def back_kernel(where, *refs):
    out, buf, out_sems = refs[8], refs[9], refs[10]
    copies = []

    def emit(k, block):
        buf[k] = block
        copies.append(started(buf.at[k], column(out, where[k], buf.shape[2]), out_sems.at[k]))

    late_slots(refs[:6], refs[6:8], *refs[11:], emit)
    for copy in copies:
        copy.wait()


def back_blocks(where, heads, near, over, accs):
    tokens, width = accs[0].shape
    ins = [*heads, *near, *over, *accs]
    scratch = [pltpu.VMEM((2, tokens, width), bf16), pltpu.SemaphoreType.DMA((2,))] + late_scratch(accs[0])
    return call(back_kernel, where, ins, [like(tokens, 4 * width)], scratch, far=(2, 4, 6, 7, 8))[0]


def place_kernel(where, a, b, _, out, sems):
    width = a.shape[1]
    copies = [started(block, column(out, where[k], width), sems.at[k]) for k, block in enumerate((a, b))]
    for copy in copies:
        copy.wait()


def place(where, blocks, back):
    return call(
        place_kernel,
        where,
        [*blocks, back],
        [like(*back.shape)],
        [pltpu.SemaphoreType.DMA((2,))],
        far=(2, 3),
        aliases={3: 0},
    )[0]


def relay_kernel(_, rest, up, down, first, second):
    first[...] = (rest[0].astype(f32) + up[0].astype(f32)).astype(bf16)
    second[...] = (rest[1].astype(f32) + down[0].astype(f32)).astype(bf16)


def other_kernel(_, own, up, down, out):
    out[...] = (own[0].astype(f32) + up[...].astype(f32) + down[1].astype(f32)).astype(bf16)


def mine_kernel(_, own, up, down, out):
    out[...] = (own[1].astype(f32) + up[1].astype(f32) + down[...].astype(f32)).T


def final_kernel(_, part, received, key_out, value_out, k_buf, v_buf, sems):
    width = k_buf.shape[1]
    k_buf[...] = part[:, :width] + received[:width].astype(f32).T
    first = started(k_buf, key_out, sems.at[0])
    v_buf[...] = part[:, width:] + received[width:].astype(f32).T
    started(v_buf, value_out, sems.at[1]).wait()
    first.wait()


def final_sum(none, part, received):
    rows, cols = received.shape
    half = (cols, rows // 2)
    return call(
        final_kernel,
        none,
        [part, received],
        [like(*half, dtype=f32)] * 2,
        [pltpu.VMEM(half, f32), pltpu.VMEM(half, f32), pltpu.SemaphoreType.DMA((2,))],
        far=(2, 3),
    )


def local(
    inputs,
    key_grad,
    value_grad,
    key_weight,
    value_weight,
    global_params,
    momentum,
    local_params,
    fragment,
    step,
    outer_rates,
):
    iy, iz, ic, ix = (lax.axis_index(a).astype(jnp.int32) for a in ("y", "z", "c", "x"))
    none = jnp.zeros((1,), jnp.int32)
    tokens_in = inputs[0]
    local_now = local_params[0]
    base = jnp.stack([
        ((iy + d) % 4) * 4 + z * 2
        for d, z in ((2, 1 - iz), (1, iz), (2, iz), (3, 1 - iz), (1, 1 - iz), (3, iz), (0, 1 - iz), (0, iz))
    ])

    weight = join(none, key_weight[0], value_weight[0])
    weight, key_part, value_part = fence((weight, key_grad[0], value_grad[0]))
    w1, w3, w2 = shift(weight, "y", -1), shift(weight, "y", -3), shift(weight, "y", 2)
    grads, pack = prepare(base + 1 - ic, tokens_in, key_part, value_part)
    pack = shift(pack, "c", 1)
    sent = local_now.astype(bf16)
    pair_sib = lax.ppermute(sent, "r", [(k, k ^ 1) for k in range(4)])

    pack, grads_b = fence((pack, grads))
    going_up, going_down, relayed, own, sib = partials(base + ic, tokens_in, grads, pack)
    h1 = shift(grads_b, "x", 1)
    pair = (sent.astype(f32) + pair_sib.astype(f32)).astype(bf16)
    pair_sib = lax.ppermute(pair, "r", [(k, k ^ 3) for k in range(4)])

    w1, w2, w3, h1, going_up, going_down = fence((w1, w2, w3, h1, going_up, going_down))
    near0, pick1, pick2, pick3 = pick(((ix - iy) % 4).reshape(1), [weight, w1, w2, w3])
    near1, near3 = shift(pick1, "x", 1), shift(pick3, "x", 3)
    over0 = shift(near0, "z", 1)
    up, down = shift(going_up, "y", 1), shift(going_down, "y", 3)

    near1, near3, over0, pick2, pair_sib = fence((near1, near3, over0, pick2, pair_sib))
    near2 = shift(pick2, "x", 2)
    over1, over3 = shift(near1, "z", 1), shift(near3, "z", 1)

    near2, up, down, over1, grads_f = fence((near2, up, down, over1, grads))
    up_o, down_m = call(relay_kernel, none, [relayed, up, down], [like(*up.shape[1:])] * 2)
    up_o, down_m = shift(up_o, "y", 1), shift(down_m, "y", 3)
    over2 = shift(near2, "z", 1)
    h3, h2 = shift(grads_f, "x", 3), shift(grads_f, "x", 2)
    own_heads, sib_heads = [grads, h1], [sib, shift(h1, "c", 1)]
    near_own, near_sib = early_slots(none, own_heads, sib_heads, [near0, near1])
    over_own, over_sib = early_slots(none, own_heads, sib_heads, [over0, over1])
    up_o, down_m, near_own, near_sib, over_own, over_sib = fence((up_o, down_m, near_own, near_sib, over_own, over_sib))
    other = call(other_kernel, none, [own, up_o, down], [like(*own.shape[1:])])[0]
    received = shift(other, "z", 1)

    h3, h2, over3, over2, other = fence((h3, h2, over3, over2, other))
    heads, near, over = [h3, h2], [near3, near2], [over3, over2]
    sib_heads = [shift(h, "c", 1) for h in heads]
    back = back_blocks(jnp.stack([iz * 2 + ic, (1 - iz) * 2 + ic]), heads, near, over, [near_own, over_own])
    sib_heads, near, over, back = fence((sib_heads, near, over, back))
    loose = loose_blocks(none, sib_heads, near, over, [near_sib, over_sib])
    loose = [shift(block, "c", 1) for block in loose]
    mine = call(mine_kernel, none, [own, up, down_m], [like(own.shape[2], own.shape[1], dtype=f32)])[0]
    total = pair.astype(f32) + pair_sib.astype(f32)
    count_frag = outer_rates.shape[0]
    chosen = (jnp.arange(count_frag, dtype=jnp.int32) == fragment[0]).astype(f32)
    warm = jnp.minimum(1.0, (step[0].astype(f32) + 1.0) / WARMUP)
    rate = jnp.sum(chosen * outer_rates) * warm
    replicas = lax.axis_size("r")
    fresh_global, fresh_momentum = outer_step(global_params, momentum, total / replicas, rate)
    fresh_local = mixing * local_now + (1.0 - mixing) * fresh_global
    fresh_global, fresh_momentum, fresh_local, back, loose, mine, received = fence(
        (fresh_global, fresh_momentum, fresh_local, back, loose, mine, received)
    )
    back = place(jnp.stack([iz * 2 + 1 - ic, (1 - iz) * 2 + 1 - ic]), loose, back)
    wgrad_k, wgrad_v = final_sum(none, mine, received)

    return (
        back[None],
        wgrad_k[None],
        wgrad_v[None],
        fresh_global,
        fresh_momentum,
        fresh_local[None],
    )


def solution(mesh):
    fine = Mesh(mesh.devices.reshape(4, 4, 2, 2, 4), ("r", "y", "z", "c", "x"))
    fsdp = ("y", "z", "c")
    split = P("r", fsdp, "x")
    in_specs = (
        P("r", fsdp, None),
        split,
        split,
        split,
        split,
        P(fsdp, "x"),
        P(fsdp, "x"),
        split,
        P(),
        P(),
        P(),
    )
    out_specs = (split, split, split, P(fsdp, "x"), P(fsdp, "x"), split)
    return jax.shard_map(local, mesh=fine, in_specs=in_specs, out_specs=out_specs, check_vma=False)
```

```python
import jax
import jax.numpy as jnp
from jax import lax
from jax.experimental import pallas as pl
from jax.experimental.pallas import tpu as pltpu
from jax.sharding import Mesh, PartitionSpec as P

WARMUP = 64


momentum_decay = 0.9
mixing = 0.5
bf16 = jnp.bfloat16
f32 = jnp.float32
VMEM_LIMIT = 16 * 1024 * 1024


def shift(a, axis, by):
    n = lax.axis_size(axis)
    return lax.ppermute(a, axis, [(i, (i + by) % n) for i in range(n)])


def outer_step(global_part, momentum_part, average, rate):
    delta = global_part - average
    fresh_momentum = momentum_decay * momentum_part + delta
    fresh_global = global_part - rate * (delta + momentum_decay * fresh_momentum)
    return (fresh_global, fresh_momentum)


fence = lax.optimization_barrier
VMEM_SPEC = pl.BlockSpec(memory_space=pltpu.VMEM)
HBM_SPEC = pl.BlockSpec(memory_space=pltpu.HBM)
SMEM_SPEC = pl.BlockSpec(memory_space=pltpu.SMEM)


def call(kernel, where, ins, outs, scratch=(), far=(), aliases=None, flops=0):
    n_in = len(ins)
    spaces = [pltpu.HBM if k in far else pltpu.VMEM for k in range(n_in + len(outs))]
    specs = [HBM_SPEC if space is pltpu.HBM else VMEM_SPEC for space in spaces]
    placed = [pltpu.with_memory_space_constraint(a, space) for a, space in zip(ins, spaces)]
    return pl.pallas_call(
        kernel,
        out_shape=[space(a.shape, a.dtype) for a, space in zip(outs, spaces[n_in:])],
        in_specs=[SMEM_SPEC] + specs[:n_in],
        out_specs=specs[n_in:],
        scratch_shapes=list(scratch),
        input_output_aliases=aliases or {},
        compiler_params=pltpu.CompilerParams(vmem_limit_bytes=VMEM_LIMIT),
        cost_estimate=pl.CostEstimate(flops=flops, bytes_accessed=0, transcendentals=0),
    )(where, *placed)


def like(*shape, dtype=bf16):
    return jax.ShapeDtypeStruct(shape, dtype)


def started(src, dst, sem):
    copy = pltpu.make_async_copy(src, dst, sem)
    copy.start()
    return copy


def column(ref, index, width):
    return ref.at[:, pl.ds(pl.multiple_of(index * width, width), width)]


def join_kernel(_, a, b, out, sems):
    width = a.shape[1]
    copies = [started(a, out.at[:, :width], sems.at[0]), started(b, out.at[:, width:], sems.at[1])]
    for copy in copies:
        copy.wait()


def join(none, a, b):
    rows, width = a.shape
    return call(join_kernel, none, [a, b], [like(rows, 2 * width)], [pltpu.SemaphoreType.DMA((2,))], far=(0, 1))[0]


def prepare_kernel(where, x, gk, gv, grads, pack, sems):
    width = gk.shape[1]
    block = pack.shape[2]
    count = pack.shape[0] - 1
    joined = [started(gk, grads.at[:, :width], sems.at[0]), started(gv, grads.at[:, width:], sems.at[1])]
    copies = [started(column(x, where[i], block), pack.at[i], sems.at[2 + i]) for i in range(count)]
    for copy in joined:
        copy.wait()
    pack[count] = grads[...]
    for copy in copies:
        copy.wait()


def prepare(where, tokens_in, gk, gv):
    rows, width = gk.shape
    count = where.shape[0]
    outs = [like(rows, 2 * width), like(count + 1, rows, 2 * width)]
    return call(prepare_kernel, where, [tokens_in, gk, gv], outs, [pltpu.SemaphoreType.DMA((2 + count,))], far=(0, 1, 2))


def partial_kernel(where, x, grads, pack, *refs):
    pairs, sib_out, (x_buf, sems) = refs[:-3], refs[-3], refs[-2:]
    width = grads.shape[1]
    outs = [ref.at[k] for ref in pairs for k in range(2)]
    sib = pack.at[len(outs)]

    def load(i):
        return started(column(x, where[i], width), x_buf.at[i % 3], sems.at[i % 3])

    loads = [load(i) for i in range(2)]
    for i, out in enumerate(outs):
        if i + 2 < len(outs):
            loads.append(load(i + 2))
        loads[i].wait()
        acc = lax.dot_general(grads[...], x_buf[i % 3], (((0,), (0,)), ((), ())), preferred_element_type=f32)
        acc = acc + lax.dot_general(sib[...], pack[i], (((0,), (0,)), ((), ())), preferred_element_type=f32)
        out[...] = acc.astype(bf16)
    sib_out[...] = sib[...]


def partials(where, tokens_in, grads, pack):
    rows, width = grads.shape
    return call(
        partial_kernel,
        where,
        [tokens_in, grads, pack],
        [like(2, width, width)] * 4 + [like(rows, width)],
        [pltpu.VMEM((3, rows, width), bf16), pltpu.SemaphoreType.DMA((3,))],
        far=(0,),
        flops=32 * rows * width * width,
    )


def pick_kernel(where, *refs):
    held, outs = refs[:4], refs[4:]
    for s in range(4):
        for d in range(4):
            @pl.when((where[0] + s) % 4 == d)
            def _(s=s, d=d):
                outs[s][...] = held[d][...]


def pick(turn, held):
    return call(pick_kernel, turn, held, [like(*held[0].shape)] * 4)


def product(lhs, rhs):
    return lax.dot_general(lhs[...], rhs[...], (((1,), (1,)), ((), ())), preferred_element_type=f32)


def early_kernel(_, *refs):
    own, sib, weights = refs[0:2], refs[2:4], refs[4:6]
    own_acc, sib_acc, buf, sems = refs[6:]
    order = [group[k] for k in range(2) for group in (weights, own, sib)]
    copies = [started(src, buf.at[i], sems.at[i]) for i, src in enumerate(order)]
    for k in range(2):
        for j, acc in enumerate((None, own_acc, sib_acc)):
            copies[3 * k + j].wait()
            if acc is not None:
                part = product(buf.at[3 * k + j], buf.at[3 * k])
                acc[...] = part if k == 0 else acc[...] + part


def early_slots(none, own, sib, weights):
    tokens, width = own[0].shape
    return call(
        early_kernel,
        none,
        [*own, *sib, *weights],
        [like(tokens, width, dtype=f32)] * 2,
        [pltpu.VMEM((6, tokens, width), bf16), pltpu.SemaphoreType.DMA((6,))],
        far=(0, 1, 2, 4, 5),
        flops=8 * tokens * width * width,
    )


def late_slots(refs, accs, w_buf, a_buf, sems, emit):
    heads, blocks = refs[0:2], (refs[2:4], refs[4:6])
    copies = [
        (started(block[0], w_buf.at[k], sems.at[0, k]), started(acc, a_buf.at[k], sems.at[1, k]))
        for k, (block, acc) in enumerate(zip(blocks, accs))
    ]
    for k, block in enumerate(blocks):
        part = product(heads[1], block[1])
        for copy in copies[k]:
            copy.wait()
        emit(k, (a_buf[k] + product(heads[0], w_buf.at[k]) + part).astype(bf16))


def late_scratch(acc):
    return [pltpu.VMEM((2, *acc.shape), bf16), pltpu.VMEM((2, *acc.shape), f32), pltpu.SemaphoreType.DMA((2, 2))]


def loose_kernel(_, *refs):
    def emit(k, block):
        refs[8 + k][...] = block

    late_slots(refs[:6], refs[6:8], *refs[10:], emit)


def loose_blocks(none, heads, near, over, accs):
    ins = [*heads, *near, *over, *accs]
    return call(loose_kernel, none, ins, [like(*accs[0].shape)] * 2, late_scratch(accs[0]), far=(2, 4, 6, 7))


def back_kernel(where, *refs):
    out, buf, out_sems = refs[8], refs[9], refs[10]
    copies = []

    def emit(k, block):
        buf[k] = block
        copies.append(started(buf.at[k], column(out, where[k], buf.shape[2]), out_sems.at[k]))

    late_slots(refs[:6], refs[6:8], *refs[11:], emit)
    for copy in copies:
        copy.wait()


def back_blocks(where, heads, near, over, accs):
    tokens, width = accs[0].shape
    ins = [*heads, *near, *over, *accs]
    scratch = [pltpu.VMEM((2, tokens, width), bf16), pltpu.SemaphoreType.DMA((2,))] + late_scratch(accs[0])
    return call(back_kernel, where, ins, [like(tokens, 4 * width)], scratch, far=(2, 4, 6, 7, 8))[0]


def relay_kernel(_, rest, up, down, first, second):
    first[...] = (rest[0].astype(f32) + up[0].astype(f32)).astype(bf16)
    second[...] = (rest[1].astype(f32) + down[0].astype(f32)).astype(bf16)


def other_kernel(_, own, up, down, out):
    out[...] = (own[0].astype(f32) + up[...].astype(f32) + down[1].astype(f32)).astype(bf16)


def mine_kernel(_, own, up, down, out):
    out[...] = (own[1].astype(f32) + up[1].astype(f32) + down[...].astype(f32)).T


def final_kernel(where, part, received, a, b, _, key_out, value_out, out, k_buf, v_buf, sems):
    cols = a.shape[1]
    copies = [started(block, column(out, where[k], cols), sems.at[k]) for k, block in enumerate((a, b))]
    width = k_buf.shape[1]
    k_buf[...] = part[:, :width] + received[:width].astype(f32).T
    copies.append(started(k_buf, key_out, sems.at[2]))
    v_buf[...] = part[:, width:] + received[width:].astype(f32).T
    copies.append(started(v_buf, value_out, sems.at[3]))
    for copy in copies:
        copy.wait()


def finish(where, part, received, blocks, back):
    rows, cols = received.shape
    half = (cols, rows // 2)
    return call(
        final_kernel,
        where,
        [part, received, *blocks, back],
        [like(*half, dtype=f32)] * 2 + [like(*back.shape)],
        [pltpu.VMEM(half, f32), pltpu.VMEM(half, f32), pltpu.SemaphoreType.DMA((4,))],
        far=(4, 5, 6, 7),
        aliases={5: 2},
    )


def local(
    inputs,
    key_grad,
    value_grad,
    key_weight,
    value_weight,
    global_params,
    momentum,
    local_params,
    fragment,
    step,
    outer_rates,
):
    iy, iz, ic, ix = (lax.axis_index(a).astype(jnp.int32) for a in ("y", "z", "c", "x"))
    none = jnp.zeros((1,), jnp.int32)
    tokens_in = inputs[0]
    local_now = local_params[0]
    base = jnp.stack([
        ((iy + d) % 4) * 4 + z * 2
        for d, z in ((2, 1 - iz), (1, iz), (2, iz), (3, 1 - iz), (1, 1 - iz), (3, iz), (0, 1 - iz), (0, iz))
    ])

    weight = join(none, key_weight[0], value_weight[0])
    weight, key_part, value_part = fence((weight, key_grad[0], value_grad[0]))
    w1, w3, w2 = shift(weight, "y", -1), shift(weight, "y", -3), shift(weight, "y", 2)
    grads, pack = prepare(base + 1 - ic, tokens_in, key_part, value_part)
    pack = shift(pack, "c", 1)
    sent = local_now.astype(bf16)
    pair_sib = lax.ppermute(sent, "r", [(k, k ^ 1) for k in range(4)])

    pack, grads_b = fence((pack, grads))
    going_up, going_down, relayed, own, sib = partials(base + ic, tokens_in, grads, pack)
    h1 = shift(grads_b, "x", 1)
    pair = (sent.astype(f32) + pair_sib.astype(f32)).astype(bf16)
    pair_sib = lax.ppermute(pair, "r", [(k, k ^ 3) for k in range(4)])

    w1, w2, w3, h1, going_up, going_down = fence((w1, w2, w3, h1, going_up, going_down))
    near0, pick1, pick2, pick3 = pick(((ix - iy) % 4).reshape(1), [weight, w1, w2, w3])
    near1, near3 = shift(pick1, "x", 1), shift(pick3, "x", 3)
    over0 = shift(near0, "z", 1)
    up, down = shift(going_up, "y", 1), shift(going_down, "y", 3)

    near1, near3, over0, pick2, pair_sib = fence((near1, near3, over0, pick2, pair_sib))
    near2 = shift(pick2, "x", 2)
    over1, over3 = shift(near1, "z", 1), shift(near3, "z", 1)

    near2, up, down, over1, grads_f = fence((near2, up, down, over1, grads))
    up_o, down_m = call(relay_kernel, none, [relayed, up, down], [like(*up.shape[1:])] * 2)
    up_o, down_m = shift(up_o, "y", 1), shift(down_m, "y", 3)
    over2 = shift(near2, "z", 1)
    h3, h2 = shift(grads_f, "x", 3), shift(grads_f, "x", 2)
    own_heads, sib_heads = [grads, h1], [sib, shift(h1, "c", 1)]
    near_own, near_sib = early_slots(none, own_heads, sib_heads, [near0, near1])
    over_own, over_sib = early_slots(none, own_heads, sib_heads, [over0, over1])
    up_o, down_m, near_own, near_sib, over_own, over_sib = fence((up_o, down_m, near_own, near_sib, over_own, over_sib))
    other = call(other_kernel, none, [own, up_o, down], [like(*own.shape[1:])])[0]
    received = shift(other, "z", 1)

    h3, h2, over3, over2, other = fence((h3, h2, over3, over2, other))
    heads, near, over = [h3, h2], [near3, near2], [over3, over2]
    sib_heads = [shift(h, "c", 1) for h in heads]
    back = back_blocks(jnp.stack([iz * 2 + ic, (1 - iz) * 2 + ic]), heads, near, over, [near_own, over_own])
    sib_heads, near, over, back = fence((sib_heads, near, over, back))
    loose = loose_blocks(none, sib_heads, near, over, [near_sib, over_sib])
    loose = [shift(block, "c", 1) for block in loose]
    mine = call(mine_kernel, none, [own, up, down_m], [like(own.shape[2], own.shape[1], dtype=f32)])[0]
    total = pair.astype(f32) + pair_sib.astype(f32)
    count_frag = outer_rates.shape[0]
    chosen = (jnp.arange(count_frag, dtype=jnp.int32) == fragment[0]).astype(f32)
    warm = jnp.minimum(1.0, (step[0].astype(f32) + 1.0) / WARMUP)
    rate = jnp.sum(chosen * outer_rates) * warm
    replicas = lax.axis_size("r")
    fresh_global, fresh_momentum = outer_step(global_params, momentum, total / replicas, rate)
    fresh_local = mixing * local_now + (1.0 - mixing) * fresh_global
    fresh_global, fresh_momentum, fresh_local, back, loose, mine, received = fence(
        (fresh_global, fresh_momentum, fresh_local, back, loose, mine, received)
    )
    places = jnp.stack([iz * 2 + 1 - ic, (1 - iz) * 2 + 1 - ic])
    wgrad_k, wgrad_v, back = finish(places, mine, received, loose, back)
    return (
        back[None],
        wgrad_k[None],
        wgrad_v[None],
        fresh_global,
        fresh_momentum,
        fresh_local[None],
    )


def solution(mesh):
    fine = Mesh(mesh.devices.reshape(4, 4, 2, 2, 4), ("r", "y", "z", "c", "x"))
    fsdp = ("y", "z", "c")
    split = P("r", fsdp, "x")
    in_specs = (
        P("r", fsdp, None),
        split,
        split,
        split,
        split,
        P(fsdp, "x"),
        P(fsdp, "x"),
        split,
        P(),
        P(),
        P(),
    )
    out_specs = (split, split, split, P(fsdp, "x"), P(fsdp, "x"), split)
    return jax.shard_map(local, mesh=fine, in_specs=in_specs, out_specs=out_specs, check_vma=False)
```
